32 devices in a mesh: mb: 4 (over y, x), feat: 8 (over z, core).
Axes of the slice: x: 2, y: 2, z: 4, core: 2. Of those that a mesh axis runs over, the one named last changes fastest.
Arguments:
- features: float32 [1024, 262144], P('feat', 'mb'), may hold values from -6 to 6
- tile_rows: int32 [768], P('mb'), may hold values from 0 to 127
- tile_cols: int32 [768], P('mb'), may hold values from 0 to 511
- tile_masks: int32 [768, 128, 128], P('mb'), may hold values 0 or 1
- weight: bfloat16 [1024, 256], replicated, may hold values from -0.5625 to 0.5625
- upstream: bfloat16 [65536, 256], P(('mb', 'feat')), may hold values from -6 to 6
Outputs:
- activation: bfloat16 [65536, 256], P(('mb', 'feat'))
- weight_grad: float32 [1024, 256], P('feat')
The draws below stay inside these ranges and needn't reach their ends.
All inputs are finite; a program needn't handle non-finite values. No bound on the sum of `tile_masks` on one device may be relied on, other than what follows from the above.
Results may differ from the reference program's by a relative error of at most 0.0063.
Values may be sent and summed in bfloat16 or wider, within the bound.
A program may use at most 192 MiB of HBM per device.

```python
import math
import jax
import jax.numpy as jnp
import numpy as np
from jax import lax

F = 1024
OUT = 256
TILE = 128
NT = 16384
NSRC = 65536
TILES = 192
SRC_ALL = 262144
TGT_ALL = 65536
TILES_ALL = 768
N_MB = 4


def plant(result, own_key, low, high):
    dims = result.shape
    place = [jax.random.randint(jax.random.fold_in(own_key, axis), (), 0, dims[axis]) for axis in range(len(dims))]
    result = result.at[tuple(place)].set(low)
    longest = dims.index(max(dims))
    place[longest] = (place[longest] + 1) % dims[longest]
    return result.at[tuple(place)].set(high)


def block_scale(own_key, extent, cuts, least, top_value):
    factor_of, own = 1.0, jax.random.fold_in(own_key, 6)
    for dim, shards_of in cuts:
        draws = jnp.exp(jax.random.uniform(jax.random.fold_in(own, dim), (shards_of,), jnp.float32, least / len(cuts), top_value / len(cuts)))
        factor_of = factor_of * jnp.repeat(draws, extent[dim] // shards_of).reshape([-1 if axis == dim else 1 for axis in range(len(extent))])
    return factor_of


def rank_bounds(count, skew):
    loads = [(1 << 20) // math.isqrt(grade ** skew) + 1 for grade in range(1, count + 1)]
    spread = 1 + sum(loads) // (1 << 30)
    return np.cumsum(np.array([max(1, weight // spread) for weight in loads]))


def skewed_ids(own_key, dims, count, slope):
    listing = rank_bounds(count, slope)
    pick = jax.random.randint(jax.random.fold_in(own_key, 1), dims, 0, int(listing[count - 1]))
    standing = jnp.searchsorted(jnp.asarray(listing, jnp.int32), pick, side="right")
    return jax.random.permutation(jax.random.fold_in(own_key, 2), count)[standing].astype(jnp.int32)


def normal_values(rng, extent, deviation, bound, cuts=(), held_as=jnp.bfloat16):
    drawn = deviation * jax.random.normal(rng, extent, jnp.float32)
    if cuts:
        drawn = drawn * block_scale(rng, extent, cuts, -0.22, 0.18)
    return jnp.clip(drawn, -bound, bound).astype(held_as)


def setup_inputs(seed: int = 0) -> dict:
    streams_of = jax.random.split(jax.random.key(seed), 7)
    return {
        "features": normal_values(streams_of[0], (F, SRC_ALL), 1.0, 6.0, ((0, 8), (1, 4)), jnp.float32),
        "tile_rows": plant(skewed_ids(streams_of[1], (TILES_ALL,), NT // TILE, 2), jax.random.fold_in(streams_of[1], 3), 0, (NT // TILE) - 1).astype(jnp.int32),
        "tile_cols": plant(jax.random.randint(streams_of[2], (TILES_ALL,), 0, NSRC // TILE), jax.random.fold_in(streams_of[2], 1), 0, (NSRC // TILE) - 1).astype(jnp.int32),
        "tile_masks": plant((jax.random.randint(streams_of[3], (TILES_ALL, TILE, TILE), 0, 16) < 1).astype(jnp.int32), jax.random.fold_in(streams_of[3], 1), 0, 1),
        "weight": normal_values(streams_of[4], (F, OUT), (3.0 / F ** 0.5), 0.5625),
        "upstream": normal_values(streams_of[5], (TGT_ALL, OUT), 1.0, 6.0, ((0, 32),)),
    }


def smooth_gate(values):
    return 0.5 * values * (1.0 + lax.erf(values * 0.7071067811865476))


def gate_slope(values):
    return 0.5 * (1.0 + lax.erf(values * 0.7071067811865476)) + values * jnp.exp(-0.5 * values * values) * 0.3989422804014327


def neighbor_mean(sources, row_index, col_index, masks):
    feat_cols = sources.shape[0]
    src_count = sources.shape[1]
    tile_size = masks.shape[1]
    row_tiles = NT // tile_size
    blocks = sources.reshape(feat_cols, src_count // tile_size, tile_size)
    picked = jnp.take(blocks, col_index, axis=1)
    weights = masks.astype(jnp.float32)
    contrib = jnp.einsum("fts,tds->tfd", picked, weights, precision=lax.Precision.HIGHEST)
    onehot = (row_index[None, :] == jnp.arange(row_tiles, dtype=jnp.int32)[:, None]).astype(jnp.float32)
    summed = jnp.einsum("rt,tfd->frd", onehot, contrib, precision=lax.Precision.HIGHEST).reshape(feat_cols, NT)
    degree = jnp.dot(onehot, jnp.sum(weights, axis=2), precision=lax.Precision.HIGHEST).reshape(NT)
    return ((sources[:, :NT] + summed) / (degree[None, :] + 1.0)).astype(jnp.bfloat16)


def reference(features, tile_rows, tile_cols, tile_masks, weight, upstream):
    outputs = []
    grad_total = jnp.zeros((F, OUT), jnp.float32)
    for member in range(N_MB):
        sources = features[:, member * NSRC:(member + 1) * NSRC]
        first_tile = member * TILES
        hidden_t = neighbor_mean(sources, tile_rows[first_tile:first_tile + TILES], tile_cols[first_tile:first_tile + TILES], tile_masks[first_tile:first_tile + TILES])
        preact = lax.dot_general(hidden_t, weight, (((0,), (0,)), ((), ())), preferred_element_type=jnp.float32)
        outputs.append(smooth_gate(preact).astype(jnp.bfloat16))
        slopes = (upstream[member * NT:(member + 1) * NT].astype(jnp.float32) * gate_slope(preact)).astype(jnp.bfloat16)
        grad_total = grad_total + jnp.dot(hidden_t, slopes, preferred_element_type=jnp.float32)
    return jnp.concatenate(outputs, 0), grad_total
```

```python
import functools
import math

import jax
import jax.numpy as jnp
from jax import lax
from jax.experimental import pallas as pl
from jax.experimental.pallas import tpu as pltpu
from jax.sharding import PartitionSpec as P

VMEM_LIMIT = 60 * 1024 * 1024
DEG_ROWS = 16


def aggregate_kernel(group, rows_ref, cols_ref, feat_ref, mask_ref, out_ref,
                     acc, own, tiles, masks, outbuf, tile_sem, mask_sem, own_sem, out_sem):
    n_tiles, tile = mask_ref.shape[0], mask_ref.shape[1]
    fl = feat_ref.shape[0]
    n_dst, chunks, _, width = out_ref.shape
    n_groups = n_tiles // group
    per_dst = chunks * width

    def fetch(g, _):
        for j in range(group):
            col = pl.multiple_of(cols_ref[g * group + j] * tile, tile)
            pltpu.make_async_copy(
                feat_ref.at[:, pl.ds(col, tile)], tiles.at[g, j], tile_sem.at[g]
            ).start()
        pltpu.make_async_copy(
            mask_ref.at[pl.ds(g * group, group)], masks.at[g], mask_sem.at[g]
        ).start()
        return 0

    lax.fori_loop(0, n_groups, fetch, 0)

    def fetch_own(d, _):
        at = pl.multiple_of(d * per_dst, per_dst)
        pltpu.make_async_copy(
            feat_ref.at[:, pl.ds(at, per_dst)], own.at[d], own_sem.at[d]
        ).start()
        return 0

    lax.fori_loop(0, n_dst, fetch_own, 0)

    def clear(i, _):
        acc[i] = jnp.zeros(acc.shape[1:], jnp.float32)
        return 0

    lax.fori_loop(0, acc.shape[0], clear, 0)

    ones = jnp.ones((DEG_ROWS, tile), jnp.bfloat16)

    def add_group(g, _):
        pltpu.make_async_copy(mask_ref.at[pl.ds(0, group)], masks.at[g], mask_sem.at[g]).wait()
        pltpu.make_async_copy(tiles.at[g], tiles.at[g], tile_sem.at[g]).wait()
        for j in range(group):
            left = jnp.concatenate([tiles[g, j].astype(jnp.bfloat16), ones], axis=0)
            right = masks[g, j].astype(jnp.float32).astype(jnp.bfloat16)
            part = lax.dot_general(
                left, right, (((1,), (1,)), ((), ())), preferred_element_type=jnp.float32
            )
            row = rows_ref[g * group + j]
            acc[row] += part
        return 0

    lax.fori_loop(0, n_groups, add_group, 0)

    blocks = width // tile

    def finish(p, _):
        d, c = p // chunks, p % chunks

        @pl.when(c == 0)
        def _():
            pltpu.make_async_copy(
                feat_ref.at[:, pl.ds(0, per_dst)], own.at[d], own_sem.at[d]
            ).wait()

        for b in range(blocks):
            r = p * blocks + b
            inv = 1.0 / (acc[r, fl:fl + 1, :] + 1.0)
            at = pl.multiple_of(c * width + b * tile, tile)
            outbuf[d, c, :, b * tile:(b + 1) * tile] = (
                (own[d, :, pl.ds(at, tile)] + acc[r, :fl, :]) * inv
            ).astype(jnp.bfloat16)
        pltpu.make_async_copy(outbuf.at[d, c], out_ref.at[d, c], out_sem).start()
        return 0

    lax.fori_loop(0, n_dst * chunks, finish, 0)
    pltpu.make_async_copy(outbuf, out_ref, out_sem).wait()


def aggregate(features, rows, cols, masks, n_dst, chunks, per_dst):
    fl = features.shape[0]
    n_tiles, tile, _ = masks.shape
    width = per_dst // chunks
    group = math.gcd(n_tiles, 8)
    n_groups = n_tiles // group
    return pl.pallas_call(
        functools.partial(aggregate_kernel, group),
        out_shape=jax.ShapeDtypeStruct((n_dst, chunks, fl, width), jnp.bfloat16),
        in_specs=[
            pl.BlockSpec(memory_space=pltpu.SMEM),
            pl.BlockSpec(memory_space=pltpu.SMEM),
            pl.BlockSpec(memory_space=pl.ANY),
            pl.BlockSpec(memory_space=pl.ANY),
        ],
        out_specs=pl.BlockSpec(memory_space=pl.ANY),
        scratch_shapes=[
            pltpu.VMEM((n_dst * per_dst // tile, fl + DEG_ROWS, tile), jnp.float32),
            pltpu.VMEM((n_dst, fl, per_dst), jnp.float32),
            pltpu.VMEM((n_groups, group, fl, tile), jnp.float32),
            pltpu.VMEM((n_groups, group, tile, tile), jnp.int32),
            pltpu.VMEM((n_dst, chunks, fl, width), jnp.bfloat16),
            pltpu.SemaphoreType.DMA((n_groups,)),
            pltpu.SemaphoreType.DMA((n_groups,)),
            pltpu.SemaphoreType.DMA((n_dst,)),
            pltpu.SemaphoreType.DMA,
        ],
        compiler_params=pltpu.CompilerParams(vmem_limit_bytes=VMEM_LIMIT),
        name="aggregate",
    )(rows, cols, features, masks)


def flip(index, offset):
    bit = 1
    while bit <= offset:
        if offset & bit:
            index = index + bit - 2 * bit * ((index // bit) % 2)
        bit *= 2
    return index


def exchange_kernel(n_feat, hid_ref, w_ref, up_ref, act_ref, grad_ref, held, send_sem, recv_sem, own_sem):
    me = lax.axis_index("feat")
    _, chunks, fl, width = hid_ref.shape
    peers = [flip(me, offset) for offset in range(n_feat - 1, 0, -1)]
    mine = pl.ds(pl.multiple_of(me * fl, fl), fl)

    barrier = pltpu.get_barrier_semaphore()
    for peer in peers:
        pl.semaphore_signal(
            barrier, inc=1, device_id={"feat": peer}, device_id_type=pl.DeviceIdType.MESH
        )
    pl.semaphore_wait(barrier, n_feat - 1)

    def send(c, slot, peer):
        return pltpu.make_async_remote_copy(
            src_ref=hid_ref.at[peer, c],
            dst_ref=held.at[c, mine],
            send_sem=send_sem.at[c, slot],
            recv_sem=recv_sem.at[c, slot],
            device_id={"feat": peer},
            device_id_type=pl.DeviceIdType.MESH,
        )

    def keep(c):
        return pltpu.make_async_copy(hid_ref.at[me, c], held.at[c, mine], own_sem.at[c])

    ahead = min(2, chunks)
    for c in range(ahead):
        for slot, peer in enumerate(peers):
            send(c, slot, peer).start()
    for c in range(chunks):
        keep(c).start()

    grad_ref[...] = jnp.zeros_like(grad_ref)

    def work(c, _):
        @pl.when(c + ahead < chunks)
        def _():
            for slot, peer in enumerate(peers):
                send(c, slot, peer).wait_send()
                send(c + ahead, slot, peer).start()

        @pl.when(c + ahead >= chunks)
        def _():
            for slot, peer in enumerate(peers):
                send(c, slot, peer).wait_send()

        keep(c).wait()
        for slot, peer in enumerate(peers):
            send(c, slot, peer).wait_recv()
        hidden = held[c]
        preact = lax.dot_general(
            hidden, w_ref[...], (((0,), (0,)), ((), ())), preferred_element_type=jnp.float32
        )
        rows = pl.ds(pl.multiple_of(c * width, width), width)
        cdf = 0.5 * (1.0 + lax.erf(preact * 0.7071067811865476))
        act_ref[rows, :] = (preact * cdf).astype(jnp.bfloat16)
        slope = cdf + preact * jnp.exp(-0.5 * preact * preact) * 0.3989422804014327
        slopes = (up_ref[rows, :].astype(jnp.float32) * slope).astype(jnp.bfloat16)
        grad_ref[...] += jnp.dot(hidden, slopes, preferred_element_type=jnp.float32)
        return 0

    lax.fori_loop(0, chunks, work, 0)


def exchange(hidden, weight, upstream, n_feat):
    _, chunks, fl, width = hidden.shape
    full, out = weight.shape
    return pl.pallas_call(
        functools.partial(exchange_kernel, n_feat),
        out_shape=(
            jax.ShapeDtypeStruct(upstream.shape, jnp.bfloat16),
            jax.ShapeDtypeStruct((full, out), jnp.float32),
        ),
        in_specs=[
            pl.BlockSpec(memory_space=pl.ANY),
            pl.BlockSpec(memory_space=pltpu.VMEM),
            pl.BlockSpec(memory_space=pltpu.VMEM),
        ],
        out_specs=(
            pl.BlockSpec(memory_space=pltpu.VMEM),
            pl.BlockSpec(memory_space=pltpu.VMEM),
        ),
        scratch_shapes=[
            pltpu.VMEM((chunks, full, width), jnp.bfloat16),
            pltpu.SemaphoreType.DMA((chunks, n_feat - 1)),
            pltpu.SemaphoreType.DMA((chunks, n_feat - 1)),
            pltpu.SemaphoreType.DMA((chunks,)),
        ],
        compiler_params=pltpu.CompilerParams(
            collective_id=0, has_side_effects=True, vmem_limit_bytes=VMEM_LIMIT
        ),
        name="exchange",
    )(hidden, weight, upstream)


def per_device(n_feat, features, tile_rows, tile_cols, tile_masks, weight, upstream):
    per_dst = upstream.shape[0]
    tile = tile_masks.shape[1]
    chunks = math.gcd(per_dst // tile, 4)
    hidden = aggregate(features, tile_rows, tile_cols, tile_masks, n_feat, chunks, per_dst)
    activation, local_grad = exchange(hidden, weight, upstream, n_feat)
    part = lax.psum_scatter(local_grad, "feat", scatter_dimension=0, tiled=True)
    return activation, lax.psum(part, "mb")


def solution(mesh):
    return jax.shard_map(
        functools.partial(per_device, mesh.shape["feat"]),
        mesh=mesh,
        in_specs=(
            P("feat", "mb"),
            P("mb"),
            P("mb"),
            P("mb", None, None),
            P(),
            P(("mb", "feat"), None),
        ),
        out_specs=(P(("mb", "feat"), None), P("feat", None)),
        check_vma=False,
    )
```

```python
import functools
import math

import jax
import jax.numpy as jnp
from jax import lax
from jax.experimental import pallas as pl
from jax.experimental.pallas import tpu as pltpu
from jax.sharding import PartitionSpec as P

VMEM_LIMIT = 60 * 1024 * 1024
DEG_ROWS = 16


def aggregate_kernel(group, rows_ref, cols_ref, feat_ref, mask_ref, out_ref,
                     acc, own, tiles, masks, outbuf, tile_sem, mask_sem, own_sem, out_sem):
    n_tiles, tile = mask_ref.shape[0], mask_ref.shape[1]
    fl = feat_ref.shape[0]
    n_dst, chunks, _, width = out_ref.shape
    n_groups = n_tiles // group
    per_dst = chunks * width

    def fetch(g, _):
        for j in range(group):
            col = pl.multiple_of(cols_ref[g * group + j] * tile, tile)
            pltpu.make_async_copy(
                feat_ref.at[:, pl.ds(col, tile)], tiles.at[g, j], tile_sem.at[g]
            ).start()
        pltpu.make_async_copy(
            mask_ref.at[pl.ds(g * group, group)], masks.at[g], mask_sem.at[g]
        ).start()
        return 0

    lax.fori_loop(0, n_groups, fetch, 0)

    def fetch_own(d, _):
        at = pl.multiple_of(d * per_dst, per_dst)
        pltpu.make_async_copy(
            feat_ref.at[:, pl.ds(at, per_dst)], own.at[d], own_sem.at[d]
        ).start()
        return 0

    lax.fori_loop(0, n_dst, fetch_own, 0)

    def clear(i, _):
        acc[i] = jnp.zeros(acc.shape[1:], jnp.float32)
        return 0

    lax.fori_loop(0, acc.shape[0], clear, 0)

    ones = jnp.ones((DEG_ROWS, tile), jnp.bfloat16)

    def add_group(g, _):
        pltpu.make_async_copy(mask_ref.at[pl.ds(0, group)], masks.at[g], mask_sem.at[g]).wait()
        pltpu.make_async_copy(tiles.at[g], tiles.at[g], tile_sem.at[g]).wait()
        for j in range(group):
            left = jnp.concatenate([tiles[g, j].astype(jnp.bfloat16), ones], axis=0)
            right = masks[g, j].astype(jnp.float32).astype(jnp.bfloat16)
            part = lax.dot_general(
                left, right, (((1,), (1,)), ((), ())), preferred_element_type=jnp.float32
            )
            row = rows_ref[g * group + j]
            acc[row] += part
        return 0

    lax.fori_loop(0, n_groups, add_group, 0)

    blocks = width // tile

    def finish(p, _):
        d, c = p // chunks, p % chunks

        @pl.when(c == 0)
        def _():
            pltpu.make_async_copy(
                feat_ref.at[:, pl.ds(0, per_dst)], own.at[d], own_sem.at[d]
            ).wait()

        for b in range(blocks):
            r = p * blocks + b
            inv = 1.0 / (acc[r, fl:fl + 1, :] + 1.0)
            at = pl.multiple_of(c * width + b * tile, tile)
            outbuf[d, c, :, b * tile:(b + 1) * tile] = (
                (own[d, :, pl.ds(at, tile)] + acc[r, :fl, :]) * inv
            ).astype(jnp.bfloat16)
        pltpu.make_async_copy(outbuf.at[d, c], out_ref.at[d, c], out_sem).start()
        return 0

    lax.fori_loop(0, n_dst * chunks, finish, 0)
    pltpu.make_async_copy(outbuf, out_ref, out_sem).wait()


def aggregate(features, rows, cols, masks, n_dst, chunks, per_dst):
    fl = features.shape[0]
    n_tiles, tile, _ = masks.shape
    width = per_dst // chunks
    group = math.gcd(n_tiles, 8)
    n_groups = n_tiles // group
    return pl.pallas_call(
        functools.partial(aggregate_kernel, group),
        out_shape=jax.ShapeDtypeStruct((n_dst, chunks, fl, width), jnp.bfloat16),
        in_specs=[
            pl.BlockSpec(memory_space=pltpu.SMEM),
            pl.BlockSpec(memory_space=pltpu.SMEM),
            pl.BlockSpec(memory_space=pl.ANY),
            pl.BlockSpec(memory_space=pl.ANY),
        ],
        out_specs=pl.BlockSpec(memory_space=pl.ANY),
        scratch_shapes=[
            pltpu.VMEM((n_dst * per_dst // tile, fl + DEG_ROWS, tile), jnp.float32),
            pltpu.VMEM((n_dst, fl, per_dst), jnp.float32),
            pltpu.VMEM((n_groups, group, fl, tile), jnp.float32),
            pltpu.VMEM((n_groups, group, tile, tile), jnp.int32),
            pltpu.VMEM((n_dst, chunks, fl, width), jnp.bfloat16),
            pltpu.SemaphoreType.DMA((n_groups,)),
            pltpu.SemaphoreType.DMA((n_groups,)),
            pltpu.SemaphoreType.DMA((n_dst,)),
            pltpu.SemaphoreType.DMA,
        ],
        compiler_params=pltpu.CompilerParams(vmem_limit_bytes=VMEM_LIMIT),
        name="aggregate",
    )(rows, cols, features, masks)


def flip(index, offset):
    bit = 1
    while bit <= offset:
        if offset & bit:
            index = index + bit - 2 * bit * ((index // bit) % 2)
        bit *= 2
    return index


def exchange_kernel(n_feat, n_mb, hid_ref, w_ref, up_ref, act_ref, grad_ref, held, total,
                    pair_in, mb_out, mb_in, line_out, line_in, parts,
                    send_sem, recv_sem, own_sem, pair_sem, mb_sem, line_sem, part_sem):
    me = lax.axis_index("feat")
    my_mb = lax.axis_index("mb")
    _, chunks, fl, width = hid_ref.shape
    pairs = n_feat // 2
    share = fl // n_mb
    wire = mb_out.dtype
    my_pair = me // 2
    my_core = me % 2
    other_core = 1 - my_core
    partner = flip(me, 1)
    peers = [flip(me, offset) for offset in range(n_feat - 1, 0, -1)]
    members = [flip(my_mb, offset) for offset in range(n_mb - 1, 0, -1)]
    order = [flip(my_pair, offset) for offset in range(pairs - 1, -1, -1)]
    mine = pl.ds(pl.multiple_of(me * fl, fl), fl)
    mesh = pl.DeviceIdType.MESH

    barrier = pltpu.get_barrier_semaphore()
    for peer in peers:
        pl.semaphore_signal(barrier, inc=1, device_id={"feat": peer}, device_id_type=mesh)
    for member in members:
        pl.semaphore_signal(barrier, inc=1, device_id={"mb": member}, device_id_type=mesh)
    pl.semaphore_wait(barrier, n_feat - 1 + n_mb - 1)

    def send(c, slot, peer):
        return pltpu.make_async_remote_copy(
            src_ref=hid_ref.at[peer, c],
            dst_ref=held.at[c, mine],
            send_sem=send_sem.at[c, slot],
            recv_sem=recv_sem.at[c, slot],
            device_id={"feat": peer},
            device_id_type=mesh,
        )

    def keep(c):
        return pltpu.make_async_copy(hid_ref.at[me, c], held.at[c, mine], own_sem.at[c])

    def to_partner(slot, pair):
        return pltpu.make_async_remote_copy(
            src_ref=total.at[pair, other_core],
            dst_ref=pair_in.at[pair],
            send_sem=pair_sem.at[0, slot],
            recv_sem=pair_sem.at[1, slot],
            device_id={"feat": partner},
            device_id_type=mesh,
        )

    def to_member(slot, turn, member, pair):
        return pltpu.make_async_remote_copy(
            src_ref=mb_out.at[member, pair],
            dst_ref=mb_in.at[my_mb, pair],
            send_sem=mb_sem.at[0, slot, turn],
            recv_sem=mb_sem.at[1, slot, turn],
            device_id={"mb": member},
            device_id_type=mesh,
        )

    def to_line(slot, pair):
        return pltpu.make_async_remote_copy(
            src_ref=line_out.at[pair],
            dst_ref=line_in.at[my_pair],
            send_sem=line_sem.at[0, slot],
            recv_sem=line_sem.at[1, slot],
            device_id={"feat": pair * 2 + my_core},
            device_id_type=mesh,
        )

    def to_copy(turn, member):
        return pltpu.make_async_remote_copy(
            src_ref=parts.at[my_mb],
            dst_ref=parts.at[my_mb],
            send_sem=part_sem.at[0, turn],
            recv_sem=part_sem.at[1, turn],
            device_id={"mb": member},
            device_id_type=mesh,
        )

    ahead = min(AHEAD, chunks)
    for c in range(ahead):
        for slot, peer in enumerate(peers):
            send(c, slot, peer).start()
    for c in range(chunks):
        keep(c).start()

    total[...] = jnp.zeros_like(total)

    def work(c, _):
        @pl.when(c + ahead < chunks)
        def _():
            for slot, peer in enumerate(peers):
                send(c, slot, peer).wait_send()
                send(c + ahead, slot, peer).start()

        @pl.when(c + ahead >= chunks)
        def _():
            for slot, peer in enumerate(peers):
                send(c, slot, peer).wait_send()

        keep(c).wait()
        for slot, peer in enumerate(peers):
            send(c, slot, peer).wait_recv()
        preact = lax.dot_general(
            held[c], w_ref[...], (((0,), (0,)), ((), ())), preferred_element_type=jnp.float32
        )
        rows = pl.ds(pl.multiple_of(c * width, width), width)
        cdf = 0.5 * (1.0 + lax.erf(preact * 0.7071067811865476))
        act_ref[rows, :] = (preact * cdf).astype(jnp.bfloat16)
        slope = cdf + preact * jnp.exp(-0.5 * preact * preact) * 0.3989422804014327
        slopes = (up_ref[rows, :].astype(jnp.float32) * slope).astype(jnp.bfloat16)
        for slot, pair in enumerate(order):
            at = pl.ds(pl.multiple_of(pair * (2 * fl), 2 * fl), 2 * fl)
            term = jnp.dot(held[c, at, :], slopes, preferred_element_type=jnp.float32)
            total[pair] += term.reshape(2, fl, term.shape[1])

            @pl.when(c == chunks - 1)
            def _():
                to_partner(slot, pair).start()

        return 0

    lax.fori_loop(0, chunks, work, 0)

    for slot, pair in enumerate(order):
        to_partner(slot, pair).wait_recv()
        pair_in[pair] += total[pair, my_core]
        for turn, member in enumerate(members):
            at = pl.ds(pl.multiple_of(member * share, share), share)
            mb_out[member, pair] = pair_in[pair, at, :].astype(wire)
            to_member(slot, turn, member, pair).start()

    at = pl.ds(pl.multiple_of(my_mb * share, share), share)
    for slot, pair in enumerate(order):
        value = pair_in[pair, at, :]
        for turn, member in enumerate(members):
            to_member(slot, turn, member, pair).wait_recv()
            value = value + mb_in[member, pair].astype(jnp.float32)
        if slot < pairs - 1:
            line_out[pair] = value.astype(wire)
            to_line(slot, pair).start()

    for slot, pair in enumerate(order[:-1]):
        to_line(slot, pair).wait_recv()
        value = value + line_in[pair].astype(jnp.float32)
    parts[my_mb] = value
    for turn, member in enumerate(members):
        to_copy(turn, member).start()

    for slot, pair in enumerate(order):
        to_partner(slot, pair).wait_send()
        for turn, member in enumerate(members):
            to_member(slot, turn, member, pair).wait_send()
    for slot, pair in enumerate(order[:-1]):
        to_line(slot, pair).wait_send()
    for turn, member in enumerate(members):
        to_copy(turn, member).wait()
    for member in range(n_mb):
        grad_ref[member * share:(member + 1) * share, :] = parts[member]


AHEAD = 2


def exchange(hidden, weight, upstream, n_feat, n_mb):
    _, chunks, fl, width = hidden.shape
    full, out = weight.shape
    pairs, share = n_feat // 2, fl // n_mb
    wire = jnp.bfloat16 if share % 16 == 0 else jnp.float32
    return pl.pallas_call(
        functools.partial(exchange_kernel, n_feat, n_mb),
        out_shape=(
            jax.ShapeDtypeStruct(upstream.shape, jnp.bfloat16),
            jax.ShapeDtypeStruct((fl, out), jnp.float32),
        ),
        in_specs=[
            pl.BlockSpec(memory_space=pl.ANY),
            pl.BlockSpec(memory_space=pltpu.VMEM),
            pl.BlockSpec(memory_space=pltpu.VMEM),
        ],
        out_specs=(
            pl.BlockSpec(memory_space=pltpu.VMEM),
            pl.BlockSpec(memory_space=pltpu.VMEM),
        ),
        scratch_shapes=[
            pltpu.VMEM((chunks, full, width), jnp.bfloat16),
            pltpu.VMEM((pairs, 2, fl, out), jnp.float32),
            pltpu.VMEM((pairs, fl, out), jnp.float32),
            pltpu.VMEM((n_mb, pairs, share, out), wire),
            pltpu.VMEM((n_mb, pairs, share, out), wire),
            pltpu.VMEM((pairs, share, out), wire),
            pltpu.VMEM((pairs, share, out), wire),
            pltpu.VMEM((n_mb, share, out), jnp.float32),
            pltpu.SemaphoreType.DMA((chunks, n_feat - 1)),
            pltpu.SemaphoreType.DMA((chunks, n_feat - 1)),
            pltpu.SemaphoreType.DMA((chunks,)),
            pltpu.SemaphoreType.DMA((2, pairs)),
            pltpu.SemaphoreType.DMA((2, pairs, n_mb - 1)),
            pltpu.SemaphoreType.DMA((2, pairs - 1)),
            pltpu.SemaphoreType.DMA((2, n_mb - 1)),
        ],
        compiler_params=pltpu.CompilerParams(
            collective_id=0, has_side_effects=True, vmem_limit_bytes=VMEM_LIMIT
        ),
        name="exchange",
    )(hidden, weight, upstream)


def per_device(n_feat, n_mb, features, tile_rows, tile_cols, tile_masks, weight, upstream):
    per_dst = upstream.shape[0]
    tile = tile_masks.shape[1]
    chunks = math.gcd(per_dst // tile, 4)
    hidden = aggregate(features, tile_rows, tile_cols, tile_masks, n_feat, chunks, per_dst)
    return exchange(hidden, weight, upstream, n_feat, n_mb)


def solution(mesh):
    return jax.shard_map(
        functools.partial(per_device, mesh.shape["feat"], mesh.shape["mb"]),
        mesh=mesh,
        in_specs=(
            P("feat", "mb"),
            P("mb"),
            P("mb"),
            P("mb", None, None),
            P(),
            P(("mb", "feat"), None),
        ),
        out_specs=(P(("mb", "feat"), None), P("feat", None)),
        check_vma=False,
    )
```

```python
import functools
import math

import jax
import jax.numpy as jnp
from jax import lax
from jax.experimental import pallas as pl
from jax.experimental.pallas import tpu as pltpu
from jax.sharding import PartitionSpec as P

VMEM_LIMIT = 60 * 1024 * 1024
DEG_ROWS = 16


def aggregate_kernel(group, rows_ref, cols_ref, feat_ref, mask_ref, out_ref,
                     acc, own, tiles, masks, outbuf, tile_sem, mask_sem, own_sem, out_sem):
    n_tiles, tile = mask_ref.shape[0], mask_ref.shape[1]
    fl = feat_ref.shape[0]
    n_dst, chunks, _, width = out_ref.shape
    n_groups = n_tiles // group
    per_dst = chunks * width

    def fetch(g, _):
        for j in range(group):
            col = pl.multiple_of(cols_ref[g * group + j] * tile, tile)
            pltpu.make_async_copy(
                feat_ref.at[:, pl.ds(col, tile)], tiles.at[g, j], tile_sem.at[g]
            ).start()
        pltpu.make_async_copy(
            mask_ref.at[pl.ds(g * group, group)], masks.at[g], mask_sem.at[g]
        ).start()
        return 0

    lax.fori_loop(0, n_groups, fetch, 0)

    def fetch_own(d, _):
        at = pl.multiple_of(d * per_dst, per_dst)
        pltpu.make_async_copy(
            feat_ref.at[:, pl.ds(at, per_dst)], own.at[d], own_sem.at[d]
        ).start()
        return 0

    lax.fori_loop(0, n_dst, fetch_own, 0)

    def clear(i, _):
        acc[i] = jnp.zeros(acc.shape[1:], jnp.float32)
        return 0

    lax.fori_loop(0, acc.shape[0], clear, 0)

    ones = jnp.ones((DEG_ROWS, tile), jnp.bfloat16)

    def add_group(g, _):
        pltpu.make_async_copy(mask_ref.at[pl.ds(0, group)], masks.at[g], mask_sem.at[g]).wait()
        pltpu.make_async_copy(tiles.at[g], tiles.at[g], tile_sem.at[g]).wait()
        for j in range(group):
            left = jnp.concatenate([tiles[g, j].astype(jnp.bfloat16), ones], axis=0)
            right = masks[g, j].astype(jnp.float32).astype(jnp.bfloat16)
            part = lax.dot_general(
                left, right, (((1,), (1,)), ((), ())), preferred_element_type=jnp.float32
            )
            row = rows_ref[g * group + j]
            acc[row] += part
        return 0

    lax.fori_loop(0, n_groups, add_group, 0)

    blocks = width // tile

    def finish(p, _):
        d, c = p // chunks, p % chunks

        @pl.when(c == 0)
        def _():
            pltpu.make_async_copy(
                feat_ref.at[:, pl.ds(0, per_dst)], own.at[d], own_sem.at[d]
            ).wait()

        for b in range(blocks):
            r = p * blocks + b
            inv = 1.0 / (acc[r, fl:fl + 1, :] + 1.0)
            at = pl.multiple_of(c * width + b * tile, tile)
            outbuf[d, c, :, b * tile:(b + 1) * tile] = (
                (own[d, :, pl.ds(at, tile)] + acc[r, :fl, :]) * inv
            ).astype(jnp.bfloat16)
        pltpu.make_async_copy(outbuf.at[d, c], out_ref.at[d, c], out_sem).start()
        return 0

    lax.fori_loop(0, n_dst * chunks, finish, 0)
    pltpu.make_async_copy(outbuf, out_ref, out_sem).wait()


def aggregate(features, rows, cols, masks, n_dst, chunks, per_dst):
    fl = features.shape[0]
    n_tiles, tile, _ = masks.shape
    width = per_dst // chunks
    group = math.gcd(n_tiles, 8)
    n_groups = n_tiles // group
    return pl.pallas_call(
        functools.partial(aggregate_kernel, group),
        out_shape=jax.ShapeDtypeStruct((n_dst, chunks, fl, width), jnp.bfloat16),
        in_specs=[
            pl.BlockSpec(memory_space=pltpu.SMEM),
            pl.BlockSpec(memory_space=pltpu.SMEM),
            pl.BlockSpec(memory_space=pl.ANY),
            pl.BlockSpec(memory_space=pl.ANY),
        ],
        out_specs=pl.BlockSpec(memory_space=pl.ANY),
        scratch_shapes=[
            pltpu.VMEM((n_dst * per_dst // tile, fl + DEG_ROWS, tile), jnp.float32),
            pltpu.VMEM((n_dst, fl, per_dst), jnp.float32),
            pltpu.VMEM((n_groups, group, fl, tile), jnp.float32),
            pltpu.VMEM((n_groups, group, tile, tile), jnp.int32),
            pltpu.VMEM((n_dst, chunks, fl, width), jnp.bfloat16),
            pltpu.SemaphoreType.DMA((n_groups,)),
            pltpu.SemaphoreType.DMA((n_groups,)),
            pltpu.SemaphoreType.DMA((n_dst,)),
            pltpu.SemaphoreType.DMA,
        ],
        compiler_params=pltpu.CompilerParams(vmem_limit_bytes=VMEM_LIMIT),
        name="aggregate",
    )(rows, cols, features, masks)


def flip(index, offset):
    bit = 1
    while bit <= offset:
        if offset & bit:
            index = index + bit - 2 * bit * ((index // bit) % 2)
        bit *= 2
    return index


def exchange_kernel(n_feat, n_mb, hid_ref, w_ref, up_ref, act_ref, grad_ref, held, total,
                    pair_in, mb_out, mb_in, line_out, line_in, parts,
                    send_sem, recv_sem, own_sem, pair_sem, mb_sem, line_sem, part_sem,
                    weight, upstream, load_sem):
    me = lax.axis_index("feat")
    my_mb = lax.axis_index("mb")
    _, chunks, fl, width = hid_ref.shape
    pairs = n_feat // 2
    share = fl // n_mb
    wire = mb_out.dtype
    my_pair = me // 2
    my_core = me % 2
    other_core = 1 - my_core
    partner = flip(me, 1)
    peers = [flip(me, offset) for offset in range(n_feat - 1, 0, -1)]
    members = [flip(my_mb, offset) for offset in range(n_mb - 1, 0, -1)]
    order = [flip(my_pair, offset) for offset in range(pairs - 1, -1, -1)]
    mine = pl.ds(pl.multiple_of(me * fl, fl), fl)
    mesh = pl.DeviceIdType.MESH

    load_weight = pltpu.make_async_copy(w_ref, weight, load_sem.at[0])
    load_upstream = pltpu.make_async_copy(up_ref, upstream, load_sem.at[1])
    load_weight.start()
    load_upstream.start()

    barrier = pltpu.get_barrier_semaphore()
    for peer in peers:
        pl.semaphore_signal(barrier, inc=1, device_id={"feat": peer}, device_id_type=mesh)
    for member in members:
        pl.semaphore_signal(barrier, inc=1, device_id={"mb": member}, device_id_type=mesh)
    pl.semaphore_wait(barrier, n_feat - 1 + n_mb - 1)

    def send(c, slot, peer):
        return pltpu.make_async_remote_copy(
            src_ref=hid_ref.at[peer, c],
            dst_ref=held.at[c, mine],
            send_sem=send_sem.at[c, slot],
            recv_sem=recv_sem.at[c, slot],
            device_id={"feat": peer},
            device_id_type=mesh,
        )

    def keep(c):
        return pltpu.make_async_copy(hid_ref.at[me, c], held.at[c, mine], own_sem.at[c])

    def to_partner(slot, pair):
        return pltpu.make_async_remote_copy(
            src_ref=total.at[pair, other_core],
            dst_ref=pair_in.at[pair],
            send_sem=pair_sem.at[0, slot],
            recv_sem=pair_sem.at[1, slot],
            device_id={"feat": partner},
            device_id_type=mesh,
        )

    def to_member(slot, turn, member, pair):
        return pltpu.make_async_remote_copy(
            src_ref=mb_out.at[member, pair],
            dst_ref=mb_in.at[my_mb, pair],
            send_sem=mb_sem.at[0, slot, turn],
            recv_sem=mb_sem.at[1, slot, turn],
            device_id={"mb": member},
            device_id_type=mesh,
        )

    def to_line(slot, pair):
        return pltpu.make_async_remote_copy(
            src_ref=line_out.at[pair],
            dst_ref=line_in.at[my_pair],
            send_sem=line_sem.at[0, slot],
            recv_sem=line_sem.at[1, slot],
            device_id={"feat": pair * 2 + my_core},
            device_id_type=mesh,
        )

    def to_copy(turn, member):
        return pltpu.make_async_remote_copy(
            src_ref=parts.at[my_mb],
            dst_ref=parts.at[my_mb],
            send_sem=part_sem.at[0, turn],
            recv_sem=part_sem.at[1, turn],
            device_id={"mb": member},
            device_id_type=mesh,
        )

    ahead = min(AHEAD, chunks)
    for c in range(ahead):
        for slot, peer in enumerate(peers):
            send(c, slot, peer).start()
    for c in range(chunks):
        keep(c).start()

    total[...] = jnp.zeros_like(total)
    load_weight.wait()
    load_upstream.wait()

    def work(c, _):
        @pl.when(c + ahead < chunks)
        def _():
            for slot, peer in enumerate(peers):
                send(c, slot, peer).wait_send()
                send(c + ahead, slot, peer).start()

        @pl.when(c + ahead >= chunks)
        def _():
            for slot, peer in enumerate(peers):
                send(c, slot, peer).wait_send()

        keep(c).wait()
        for slot, peer in enumerate(peers):
            send(c, slot, peer).wait_recv()
        preact = lax.dot_general(
            held[c], weight[...], (((0,), (0,)), ((), ())), preferred_element_type=jnp.float32
        )
        rows = pl.ds(pl.multiple_of(c * width, width), width)
        cdf = 0.5 * (1.0 + lax.erf(preact * 0.7071067811865476))
        act_ref[rows, :] = (preact * cdf).astype(jnp.bfloat16)
        slope = cdf + preact * jnp.exp(-0.5 * preact * preact) * 0.3989422804014327
        slopes = (upstream[rows, :].astype(jnp.float32) * slope).astype(jnp.bfloat16)
        for slot, pair in enumerate(order):
            at = pl.ds(pl.multiple_of(pair * (2 * fl), 2 * fl), 2 * fl)
            term = jnp.dot(held[c, at, :], slopes, preferred_element_type=jnp.float32)
            total[pair] += term.reshape(2, fl, term.shape[1])

            @pl.when(c == chunks - 1)
            def _():
                to_partner(slot, pair).start()

        return 0

    lax.fori_loop(0, chunks, work, 0)

    for slot, pair in enumerate(order):
        to_partner(slot, pair).wait_recv()
        pair_in[pair] += total[pair, my_core]
        for turn, member in enumerate(members):
            at = pl.ds(pl.multiple_of(member * share, share), share)
            mb_out[member, pair] = pair_in[pair, at, :].astype(wire)
            to_member(slot, turn, member, pair).start()

    at = pl.ds(pl.multiple_of(my_mb * share, share), share)
    for slot, pair in enumerate(order):
        value = pair_in[pair, at, :]
        for turn, member in enumerate(members):
            to_member(slot, turn, member, pair).wait_recv()
            value = value + mb_in[member, pair].astype(jnp.float32)
        if slot < pairs - 1:
            line_out[pair] = value.astype(wire)
            to_line(slot, pair).start()

    for slot, pair in enumerate(order[:-1]):
        to_line(slot, pair).wait_recv()
        value = value + line_in[pair].astype(jnp.float32)
    parts[my_mb] = value
    for turn, member in enumerate(members):
        to_copy(turn, member).start()

    for slot, pair in enumerate(order):
        to_partner(slot, pair).wait_send()
        for turn, member in enumerate(members):
            to_member(slot, turn, member, pair).wait_send()
    for slot, pair in enumerate(order[:-1]):
        to_line(slot, pair).wait_send()
    for turn, member in enumerate(members):
        to_copy(turn, member).wait()
    for member in range(n_mb):
        grad_ref[member * share:(member + 1) * share, :] = parts[member]


AHEAD = 2


def exchange(hidden, weight, upstream, n_feat, n_mb):
    _, chunks, fl, width = hidden.shape
    full, out = weight.shape
    pairs, share = n_feat // 2, fl // n_mb
    wire = jnp.bfloat16 if share % 16 == 0 else jnp.float32
    return pl.pallas_call(
        functools.partial(exchange_kernel, n_feat, n_mb),
        out_shape=(
            jax.ShapeDtypeStruct(upstream.shape, jnp.bfloat16),
            jax.ShapeDtypeStruct((fl, out), jnp.float32),
        ),
        in_specs=[
            pl.BlockSpec(memory_space=pl.ANY),
            pl.BlockSpec(memory_space=pl.ANY),
            pl.BlockSpec(memory_space=pl.ANY),
        ],
        out_specs=(
            pl.BlockSpec(memory_space=pltpu.VMEM),
            pl.BlockSpec(memory_space=pltpu.VMEM),
        ),
        scratch_shapes=[
            pltpu.VMEM((chunks, full, width), jnp.bfloat16),
            pltpu.VMEM((pairs, 2, fl, out), jnp.float32),
            pltpu.VMEM((pairs, fl, out), jnp.float32),
            pltpu.VMEM((n_mb, pairs, share, out), wire),
            pltpu.VMEM((n_mb, pairs, share, out), wire),
            pltpu.VMEM((pairs, share, out), wire),
            pltpu.VMEM((pairs, share, out), wire),
            pltpu.VMEM((n_mb, share, out), jnp.float32),
            pltpu.SemaphoreType.DMA((chunks, n_feat - 1)),
            pltpu.SemaphoreType.DMA((chunks, n_feat - 1)),
            pltpu.SemaphoreType.DMA((chunks,)),
            pltpu.SemaphoreType.DMA((2, pairs)),
            pltpu.SemaphoreType.DMA((2, pairs, n_mb - 1)),
            pltpu.SemaphoreType.DMA((2, pairs - 1)),
            pltpu.SemaphoreType.DMA((2, n_mb - 1)),
            pltpu.VMEM(weight.shape, weight.dtype),
            pltpu.VMEM(upstream.shape, upstream.dtype),
            pltpu.SemaphoreType.DMA((2,)),
        ],
        compiler_params=pltpu.CompilerParams(
            collective_id=0, has_side_effects=True, vmem_limit_bytes=VMEM_LIMIT
        ),
        name="exchange",
    )(hidden, weight, upstream)


def hand_over_kernel(act_ref, grad_ref, act_out, grad_out, act, grad, sem):
    loads, stores = [], []
    step = act.shape[1]
    for k in range(act.shape[0]):
        rows = pl.ds(k * step, step)
        loads.append(pltpu.make_async_copy(act_ref.at[rows], act.at[k], sem.at[0, k]))
        stores.append(pltpu.make_async_copy(act.at[k], act_out.at[rows], sem.at[1, k]))
    last = act.shape[0]
    loads.append(pltpu.make_async_copy(grad_ref, grad, sem.at[0, last]))
    stores.append(pltpu.make_async_copy(grad, grad_out, sem.at[1, last]))
    for load in loads:
        load.start()
    for load, store in zip(loads, stores):
        load.wait()
        store.start()
    for store in stores:
        store.wait()


def hand_over(activation, grad):
    anywhere = pl.BlockSpec(memory_space=pl.ANY)
    rows, cols = activation.shape
    cuts = 4
    return pl.pallas_call(
        hand_over_kernel,
        out_shape=(
            jax.ShapeDtypeStruct(activation.shape, activation.dtype),
            jax.ShapeDtypeStruct(grad.shape, grad.dtype),
        ),
        in_specs=[anywhere, anywhere],
        out_specs=(anywhere, anywhere),
        scratch_shapes=[
            pltpu.VMEM((cuts, rows // cuts, cols), activation.dtype),
            pltpu.VMEM(grad.shape, grad.dtype),
            pltpu.SemaphoreType.DMA((2, cuts + 1)),
        ],
        name="hand_over",
    )(activation, grad)


def per_device(n_feat, n_mb, features, tile_rows, tile_cols, tile_masks, weight, upstream):
    per_dst = upstream.shape[0]
    tile = tile_masks.shape[1]
    chunks = math.gcd(per_dst // tile, 4)
    hidden = aggregate(features, tile_rows, tile_cols, tile_masks, n_feat, chunks, per_dst)
    return hand_over(*exchange(hidden, weight, upstream, n_feat, n_mb))


def solution(mesh):
    return jax.shard_map(
        functools.partial(per_device, mesh.shape["feat"], mesh.shape["mb"]),
        mesh=mesh,
        in_specs=(
            P("feat", "mb"),
            P("mb"),
            P("mb"),
            P("mb", None, None),
            P(),
            P(("mb", "feat"), None),
        ),
        out_specs=(P(("mb", "feat"), None), P("feat", None)),
        check_vma=False,
    )
```

```python
import functools
import math

import jax
import jax.numpy as jnp
from jax import lax
from jax.experimental import pallas as pl
from jax.experimental.pallas import tpu as pltpu
from jax.sharding import PartitionSpec as P

VMEM_LIMIT = 60 * 1024 * 1024
DEG_ROWS = 16


def aggregate_kernel(group, rows_ref, cols_ref, feat_ref, mask_ref, out_ref,
                     acc, own, tiles, masks, outbuf, tile_sem, mask_sem, own_sem, out_sem):
    n_tiles, tile = mask_ref.shape[0], mask_ref.shape[1]
    fl = feat_ref.shape[0]
    n_dst, chunks, _, width = out_ref.shape
    n_groups = n_tiles // group
    per_dst = chunks * width

    def fetch(g, _):
        for j in range(group):
            col = pl.multiple_of(cols_ref[g * group + j] * tile, tile)
            pltpu.make_async_copy(
                feat_ref.at[:, pl.ds(col, tile)], tiles.at[g, j], tile_sem.at[g]
            ).start()
        pltpu.make_async_copy(
            mask_ref.at[pl.ds(g * group, group)], masks.at[g], mask_sem.at[g]
        ).start()
        return 0

    early = min(n_groups, 8)
    lax.fori_loop(0, early, fetch, 0)

    def fetch_own(d, _):
        at = pl.multiple_of(d * per_dst, per_dst)
        pltpu.make_async_copy(
            feat_ref.at[:, pl.ds(at, per_dst)], own.at[d], own_sem.at[d]
        ).start()
        return 0

    lax.fori_loop(0, n_dst, fetch_own, 0)

    def clear(i, _):
        acc[i] = jnp.zeros(acc.shape[1:], jnp.float32)
        return 0

    lax.fori_loop(0, acc.shape[0], clear, 0)

    ones = jnp.ones((DEG_ROWS, tile), jnp.bfloat16)

    def add_group(g, _):
        @pl.when(g + early < n_groups)
        def _():
            fetch(g + early, 0)

        pltpu.make_async_copy(mask_ref.at[pl.ds(0, group)], masks.at[g], mask_sem.at[g]).wait()
        pltpu.make_async_copy(tiles.at[g], tiles.at[g], tile_sem.at[g]).wait()
        for j in range(group):
            left = jnp.concatenate([tiles[g, j].astype(jnp.bfloat16), ones], axis=0)
            right = masks[g, j].astype(jnp.float32).astype(jnp.bfloat16)
            part = lax.dot_general(
                left, right, (((1,), (1,)), ((), ())), preferred_element_type=jnp.float32
            )
            row = rows_ref[g * group + j]
            acc[row] += part
        return 0

    lax.fori_loop(0, n_groups, add_group, 0)

    blocks = width // tile

    def finish(p, _):
        d, c = p // chunks, p % chunks

        @pl.when(c == 0)
        def _():
            pltpu.make_async_copy(
                feat_ref.at[:, pl.ds(0, per_dst)], own.at[d], own_sem.at[d]
            ).wait()

        for b in range(blocks):
            r = p * blocks + b
            inv = 1.0 / (acc[r, fl:fl + 1, :] + 1.0)
            at = pl.multiple_of(c * width + b * tile, tile)
            outbuf[d, c, :, b * tile:(b + 1) * tile] = (
                (own[d, :, pl.ds(at, tile)] + acc[r, :fl, :]) * inv
            ).astype(jnp.bfloat16)
        pltpu.make_async_copy(outbuf.at[d, c], out_ref.at[d, c], out_sem).start()
        return 0

    lax.fori_loop(0, n_dst * chunks, finish, 0)
    pltpu.make_async_copy(outbuf, out_ref, out_sem).wait()


def aggregate(features, rows, cols, masks, n_dst, chunks, per_dst):
    fl = features.shape[0]
    n_tiles, tile, _ = masks.shape
    width = per_dst // chunks
    group = math.gcd(n_tiles, 8)
    n_groups = n_tiles // group
    return pl.pallas_call(
        functools.partial(aggregate_kernel, group),
        out_shape=jax.ShapeDtypeStruct((n_dst, chunks, fl, width), jnp.bfloat16),
        in_specs=[
            pl.BlockSpec(memory_space=pltpu.SMEM),
            pl.BlockSpec(memory_space=pltpu.SMEM),
            pl.BlockSpec(memory_space=pl.ANY),
            pl.BlockSpec(memory_space=pl.ANY),
        ],
        out_specs=pl.BlockSpec(memory_space=pl.ANY),
        scratch_shapes=[
            pltpu.VMEM((n_dst * per_dst // tile, fl + DEG_ROWS, tile), jnp.float32),
            pltpu.VMEM((n_dst, fl, per_dst), jnp.float32),
            pltpu.VMEM((n_groups, group, fl, tile), jnp.float32),
            pltpu.VMEM((n_groups, group, tile, tile), jnp.int32),
            pltpu.VMEM((n_dst, chunks, fl, width), jnp.bfloat16),
            pltpu.SemaphoreType.DMA((n_groups,)),
            pltpu.SemaphoreType.DMA((n_groups,)),
            pltpu.SemaphoreType.DMA((n_dst,)),
            pltpu.SemaphoreType.DMA,
        ],
        compiler_params=pltpu.CompilerParams(vmem_limit_bytes=VMEM_LIMIT),
        name="aggregate",
    )(rows, cols, features, masks)


def flip(index, offset):
    bit = 1
    while bit <= offset:
        if offset & bit:
            index = index + bit - 2 * bit * ((index // bit) % 2)
        bit *= 2
    return index


def exchange_kernel(n_feat, n_mb, hid_ref, w_ref, up_ref, act_ref, grad_ref, held, total,
                    pair_in, mb_out, mb_in, line_out, line_in, parts,
                    send_sem, recv_sem, own_sem, pair_sem, mb_sem, line_sem, part_sem,
                    weight, upstream, load_sem):
    me = lax.axis_index("feat")
    my_mb = lax.axis_index("mb")
    _, chunks, fl, width = hid_ref.shape
    pairs = n_feat // 2
    share = fl // n_mb
    wire = mb_out.dtype
    my_pair = me // 2
    my_core = me % 2
    other_core = 1 - my_core
    partner = flip(me, 1)
    peers = [flip(me, offset) for offset in range(n_feat - 1, 0, -1)]
    members = [flip(my_mb, offset) for offset in range(n_mb - 1, 0, -1)]
    order = [flip(my_pair, offset) for offset in range(pairs - 1, -1, -1)]
    mine = pl.ds(pl.multiple_of(me * fl, fl), fl)
    mesh = pl.DeviceIdType.MESH

    load_weight = pltpu.make_async_copy(w_ref, weight, load_sem.at[0])
    load_upstream = pltpu.make_async_copy(up_ref, upstream, load_sem.at[1])
    load_weight.start()
    load_upstream.start()

    barrier = pltpu.get_barrier_semaphore()
    for peer in peers:
        pl.semaphore_signal(barrier, inc=1, device_id={"feat": peer}, device_id_type=mesh)
    for member in members:
        pl.semaphore_signal(barrier, inc=1, device_id={"mb": member}, device_id_type=mesh)
    pl.semaphore_wait(barrier, n_feat - 1 + n_mb - 1)

    def send(c, slot, peer):
        return pltpu.make_async_remote_copy(
            src_ref=hid_ref.at[peer, c],
            dst_ref=held.at[c, mine],
            send_sem=send_sem.at[c, slot],
            recv_sem=recv_sem.at[c, slot],
            device_id={"feat": peer},
            device_id_type=mesh,
        )

    def keep(c):
        return pltpu.make_async_copy(hid_ref.at[me, c], held.at[c, mine], own_sem.at[c])

    def to_partner(slot, pair):
        return pltpu.make_async_remote_copy(
            src_ref=total.at[pair, other_core],
            dst_ref=pair_in.at[pair],
            send_sem=pair_sem.at[0, slot],
            recv_sem=pair_sem.at[1, slot],
            device_id={"feat": partner},
            device_id_type=mesh,
        )

    def to_member(slot, turn, member, pair):
        return pltpu.make_async_remote_copy(
            src_ref=mb_out.at[member, pair],
            dst_ref=mb_in.at[my_mb, pair],
            send_sem=mb_sem.at[0, slot, turn],
            recv_sem=mb_sem.at[1, slot, turn],
            device_id={"mb": member},
            device_id_type=mesh,
        )

    def to_line(slot, pair):
        return pltpu.make_async_remote_copy(
            src_ref=line_out.at[pair],
            dst_ref=line_in.at[my_pair],
            send_sem=line_sem.at[0, slot],
            recv_sem=line_sem.at[1, slot],
            device_id={"feat": pair * 2 + my_core},
            device_id_type=mesh,
        )

    def to_copy(turn, member):
        return pltpu.make_async_remote_copy(
            src_ref=parts.at[my_mb],
            dst_ref=parts.at[my_mb],
            send_sem=part_sem.at[0, turn],
            recv_sem=part_sem.at[1, turn],
            device_id={"mb": member},
            device_id_type=mesh,
        )

    ahead = min(AHEAD, chunks)
    for c in range(ahead):
        for slot, peer in enumerate(peers):
            send(c, slot, peer).start()
    for c in range(chunks):
        keep(c).start()

    total[...] = jnp.zeros_like(total)
    load_weight.wait()
    load_upstream.wait()

    def work(c, _):
        @pl.when(c + ahead < chunks)
        def _():
            for slot, peer in enumerate(peers):
                send(c, slot, peer).wait_send()
                send(c + ahead, slot, peer).start()

        @pl.when(c + ahead >= chunks)
        def _():
            for slot, peer in enumerate(peers):
                send(c, slot, peer).wait_send()

        keep(c).wait()
        for slot, peer in enumerate(peers):
            send(c, slot, peer).wait_recv()
        preact = lax.dot_general(
            held[c], weight[...], (((0,), (0,)), ((), ())), preferred_element_type=jnp.float32
        )
        rows = pl.ds(pl.multiple_of(c * width, width), width)
        cdf = 0.5 * (1.0 + lax.erf(preact * 0.7071067811865476))
        act_ref[rows, :] = (preact * cdf).astype(jnp.bfloat16)
        slope = cdf + preact * jnp.exp(-0.5 * preact * preact) * 0.3989422804014327
        slopes = (upstream[rows, :].astype(jnp.float32) * slope).astype(jnp.bfloat16)
        for slot, pair in enumerate(order):
            at = pl.ds(pl.multiple_of(pair * (2 * fl), 2 * fl), 2 * fl)
            term = jnp.dot(held[c, at, :], slopes, preferred_element_type=jnp.float32)
            total[pair] += term.reshape(2, fl, term.shape[1])

            @pl.when(c == chunks - 1)
            def _():
                to_partner(slot, pair).start()

        return 0

    lax.fori_loop(0, chunks, work, 0)

    for slot, pair in enumerate(order):
        to_partner(slot, pair).wait_recv()
        pair_in[pair] += total[pair, my_core]
        for turn, member in enumerate(members):
            at = pl.ds(pl.multiple_of(member * share, share), share)
            mb_out[member, pair] = pair_in[pair, at, :].astype(wire)
            to_member(slot, turn, member, pair).start()

    at = pl.ds(pl.multiple_of(my_mb * share, share), share)
    for slot, pair in enumerate(order):
        value = pair_in[pair, at, :]
        for turn, member in enumerate(members):
            to_member(slot, turn, member, pair).wait_recv()
            value = value + mb_in[member, pair].astype(jnp.float32)
        if slot < pairs - 1:
            line_out[pair] = value.astype(wire)
            to_line(slot, pair).start()

    for slot, pair in enumerate(order[:-1]):
        to_line(slot, pair).wait_recv()
        value = value + line_in[pair].astype(jnp.float32)
    parts[my_mb] = value
    for turn, member in enumerate(members):
        to_copy(turn, member).start()

    for slot, pair in enumerate(order):
        to_partner(slot, pair).wait_send()
        for turn, member in enumerate(members):
            to_member(slot, turn, member, pair).wait_send()
    for slot, pair in enumerate(order[:-1]):
        to_line(slot, pair).wait_send()
    for turn, member in enumerate(members):
        to_copy(turn, member).wait()
    for member in range(n_mb):
        grad_ref[member * share:(member + 1) * share, :] = parts[member]


AHEAD = 2


def exchange(hidden, weight, upstream, n_feat, n_mb):
    _, chunks, fl, width = hidden.shape
    full, out = weight.shape
    pairs, share = n_feat // 2, fl // n_mb
    wire = jnp.bfloat16 if share % 16 == 0 else jnp.float32
    return pl.pallas_call(
        functools.partial(exchange_kernel, n_feat, n_mb),
        out_shape=(
            jax.ShapeDtypeStruct(upstream.shape, jnp.bfloat16),
            jax.ShapeDtypeStruct((fl, out), jnp.float32),
        ),
        in_specs=[
            pl.BlockSpec(memory_space=pl.ANY),
            pl.BlockSpec(memory_space=pl.ANY),
            pl.BlockSpec(memory_space=pl.ANY),
        ],
        out_specs=(
            pl.BlockSpec(memory_space=pltpu.VMEM),
            pl.BlockSpec(memory_space=pltpu.VMEM),
        ),
        scratch_shapes=[
            pltpu.VMEM((chunks, full, width), jnp.bfloat16),
            pltpu.VMEM((pairs, 2, fl, out), jnp.float32),
            pltpu.VMEM((pairs, fl, out), jnp.float32),
            pltpu.VMEM((n_mb, pairs, share, out), wire),
            pltpu.VMEM((n_mb, pairs, share, out), wire),
            pltpu.VMEM((pairs, share, out), wire),
            pltpu.VMEM((pairs, share, out), wire),
            pltpu.VMEM((n_mb, share, out), jnp.float32),
            pltpu.SemaphoreType.DMA((chunks, n_feat - 1)),
            pltpu.SemaphoreType.DMA((chunks, n_feat - 1)),
            pltpu.SemaphoreType.DMA((chunks,)),
            pltpu.SemaphoreType.DMA((2, pairs)),
            pltpu.SemaphoreType.DMA((2, pairs, n_mb - 1)),
            pltpu.SemaphoreType.DMA((2, pairs - 1)),
            pltpu.SemaphoreType.DMA((2, n_mb - 1)),
            pltpu.VMEM(weight.shape, weight.dtype),
            pltpu.VMEM(upstream.shape, upstream.dtype),
            pltpu.SemaphoreType.DMA((2,)),
        ],
        compiler_params=pltpu.CompilerParams(
            collective_id=0, has_side_effects=True, vmem_limit_bytes=VMEM_LIMIT
        ),
        name="exchange",
    )(hidden, weight, upstream)


def hand_over_kernel(act_ref, grad_ref, act_out, grad_out, act, grad, sem):
    loads, stores = [], []
    step = act.shape[1]
    for k in range(act.shape[0]):
        rows = pl.ds(k * step, step)
        loads.append(pltpu.make_async_copy(act_ref.at[rows], act.at[k], sem.at[0, k]))
        stores.append(pltpu.make_async_copy(act.at[k], act_out.at[rows], sem.at[1, k]))
    last = act.shape[0]
    loads.append(pltpu.make_async_copy(grad_ref, grad, sem.at[0, last]))
    stores.append(pltpu.make_async_copy(grad, grad_out, sem.at[1, last]))
    for load in loads:
        load.start()
    for load, store in zip(loads, stores):
        load.wait()
        store.start()
    for store in stores:
        store.wait()


def hand_over(activation, grad):
    anywhere = pl.BlockSpec(memory_space=pl.ANY)
    rows, cols = activation.shape
    cuts = 4
    return pl.pallas_call(
        hand_over_kernel,
        out_shape=(
            jax.ShapeDtypeStruct(activation.shape, activation.dtype),
            jax.ShapeDtypeStruct(grad.shape, grad.dtype),
        ),
        in_specs=[anywhere, anywhere],
        out_specs=(anywhere, anywhere),
        scratch_shapes=[
            pltpu.VMEM((cuts, rows // cuts, cols), activation.dtype),
            pltpu.VMEM(grad.shape, grad.dtype),
            pltpu.SemaphoreType.DMA((2, cuts + 1)),
        ],
        name="hand_over",
    )(activation, grad)


def per_device(n_feat, n_mb, features, tile_rows, tile_cols, tile_masks, weight, upstream):
    per_dst = upstream.shape[0]
    tile = tile_masks.shape[1]
    chunks = math.gcd(per_dst // tile, 4)
    hidden = aggregate(features, tile_rows, tile_cols, tile_masks, n_feat, chunks, per_dst)
    return hand_over(*exchange(hidden, weight, upstream, n_feat, n_mb))


def solution(mesh):
    return jax.shard_map(
        functools.partial(per_device, mesh.shape["feat"], mesh.shape["mb"]),
        mesh=mesh,
        in_specs=(
            P("feat", "mb"),
            P("mb"),
            P("mb"),
            P("mb", None, None),
            P(),
            P(("mb", "feat"), None),
        ),
        out_specs=(P(("mb", "feat"), None), P("feat", None)),
        check_vma=False,
    )
```
